32 devices in a mesh: pix: 2 (over y), date: 16 (over z, x, core).
Axes of the slice: x: 2, y: 2, z: 4, core: 2. Of those that a mesh axis runs over, the one named last changes fastest.
Arguments:
- pixel_factors: float32 [8192, 256], P(('pix', 'date')), may hold values from -1.5 to 1.5
- date_factors: float32 [4096, 256], P('date'), may hold values from -1.5 to 1.5
- block_ids: int32 [2, 16, 2, 80], P('pix', 'date'), may hold values from 0 to 31, as said below
- block_counts: int32 [2, 16], P('pix', 'date'), may hold values from 20 to 80, as said below
- block_values: bfloat16 [2, 16, 80, 8192], P('pix', 'date'), may hold values from -6 to 6
- block_weights: bfloat16 [2, 16, 80, 8192], P('pix', 'date'), may hold values from 0 to 1
Outputs:
- pixel_out: float32 [8192, 256], P(('pix', 'date'))
- date_out: float32 [4096, 256], P('date')
The draws below stay inside these ranges and needn't reach their ends.
Inputs may be any that keep to these rules, and one draw needn't show every extreme that they name: block_ids[p, q, 0, s] is a row-block below 32 and block_ids[p, q, 1, s] a date-block below 4; the 80 pairs of one device are distinct, including those beyond its count. `block_counts`: some device holds exactly 80 observed blocks.
All inputs are finite; a program needn't handle non-finite values.
Results may differ from the reference program's by a relative error of at most 0.01.
Values may be sent and summed in bfloat16 or wider, within the bound.
No kernel may reach another device: no remote copies, remote signals or barrier semaphores. Data moves between devices by JAX's collectives and lax.ppermute only.
A program may use at most 128 MiB of HBM per device.

```python
import jax
import jax.numpy as jnp
from jax import lax

RANK = 256
DATE_DEV = 256
STEPS = 2
GROUP_ROWS = 4096
PIXELS = 8192
DATES = 4096
SLOTS = 128
BLOCKS_MAX = 80
N_PIX = 2
N_DATE = 16


def draw_block_ids(key, part):
    key = jax.random.fold_in(key, 11)
    device_keys = jax.random.split(key, N_PIX * N_DATE)
    orders = jax.vmap(lambda k: jax.random.permutation(k, SLOTS))(device_keys)[:, :BLOCKS_MAX]
    date_blocks = DATE_DEV // 64
    row_part = orders // date_blocks
    date_part = orders % date_blocks
    stacked = jnp.stack([row_part, date_part], axis=1)
    return stacked.reshape(N_PIX, N_DATE, 2, BLOCKS_MAX).astype(jnp.int32)


def draw_block_counts(key, part):
    key = jax.random.fold_in(key, 23)
    count_key, place_key = jax.random.split(key)
    counts = jax.random.randint(count_key, (N_PIX * N_DATE,), BLOCKS_MAX // 4, BLOCKS_MAX + 1)
    fullest = jax.random.randint(place_key, (), 0, N_PIX * N_DATE)
    counts = counts.at[fullest].set(BLOCKS_MAX)
    return counts.reshape(N_PIX, N_DATE).astype(jnp.int32)


def draw_block_weights(key, part):
    key = jax.random.fold_in(key, 37)
    cloud_key, level_key = jax.random.split(key)
    shape = (N_PIX, N_DATE, BLOCKS_MAX, 8192)
    cloudy = jax.random.uniform(cloud_key, shape, jnp.float32) < 0.3
    level = jnp.exp(jax.random.uniform(level_key, shape, jnp.float32, jnp.log(0.25), 0.0))
    return jnp.where(cloudy, 0.0, level).astype(jnp.bfloat16)


def levels(stream_key, extent, cuts, least, largest):
    level, own = 1.0, jax.random.fold_in(stream_key, 6)
    for dim, shards_of in cuts:
        heights = jnp.exp(jax.random.uniform(jax.random.fold_in(own, dim), (shards_of,), jnp.float32, least / len(cuts), largest / len(cuts)))
        level = level * jnp.repeat(heights, extent[dim] // shards_of).reshape([-1 if axis == dim else 1 for axis in range(len(extent))])
    return level


def gaussian(stream_key, dims, scale, limit, shards=(), kind=jnp.bfloat16):
    gain = levels(stream_key, dims, shards, -0.22, 0.18) if shards else 1.0
    values = jax.random.normal(stream_key, dims, jnp.float32) * scale * gain
    return jnp.minimum(jnp.maximum(values, -limit), limit).astype(kind)


def setup_inputs(seed: int = 0) -> dict:
    streams_of = jax.random.split(jax.random.key(seed), 7)
    pixel_factors = gaussian(streams_of[0], (PIXELS, RANK), 0.25, 1.5, ((0, 32),), jnp.float32)
    date_factors = gaussian(streams_of[1], (DATES, RANK), 0.25, 1.5, ((0, 16),), jnp.float32)
    block_ids = draw_block_ids(jax.random.fold_in(streams_of[6], 71), 0)
    block_counts = draw_block_counts(jax.random.fold_in(streams_of[6], 71), 0)
    block_values = gaussian(streams_of[4], (N_PIX, N_DATE, BLOCKS_MAX, 8192), 1.0, 6.0, ((0, 2), (1, 16)))
    block_weights = draw_block_weights(jax.random.fold_in(streams_of[6], 71), 0)
    return {"pixel_factors": pixel_factors, "date_factors": date_factors, "block_ids": block_ids, "block_counts": block_counts, "block_values": block_values, "block_weights": block_weights}


DECAY = 0.05
STEP_SCALE = 48.0


def place_panel(block_list, filled, tiles):
    slots = tiles.shape[0]
    valid = (jnp.arange(slots, dtype=jnp.int32) < filled).astype(jnp.float32)
    blocks = tiles.reshape(slots, 128, 64).astype(jnp.float32) * valid[:, None, None]
    dense = jnp.zeros((GROUP_ROWS // 128, DATE_DEV // 64, 128, 64), jnp.float32)
    dense = dense.at[block_list[0].astype(jnp.int32), block_list[1].astype(jnp.int32)].add(blocks)
    return jnp.transpose(dense, (0, 2, 1, 3)).reshape(GROUP_ROWS, DATE_DEV).astype(jnp.bfloat16)


def one_step(pixel_now, dates_now, block_ids, block_counts, block_values, block_weights):
    groups_bf = pixel_now.astype(jnp.bfloat16).reshape(N_PIX, GROUP_ROWS, RANK)
    dates_bf = dates_now.astype(jnp.bfloat16).reshape(N_DATE, DATE_DEV, RANK)

    def per_group(date_sum, inputs):
        group_bf, id_row, count_row, value_row, weight_row = inputs

        def per_device(row_sum, dev_inputs):
            local_dates, block_list, filled, values, weights = dev_inputs
            observed = place_panel(block_list, filled, values)
            weights_panel = place_panel(block_list, filled, weights)
            predicted = jnp.dot(group_bf, local_dates.T, preferred_element_type=jnp.float32)
            errors = (weights_panel.astype(jnp.float32) * (predicted - observed.astype(jnp.float32))).astype(jnp.bfloat16)
            row_term = jnp.dot(errors, local_dates, preferred_element_type=jnp.float32).astype(jnp.bfloat16)
            row_term = lax.optimization_barrier(row_term).astype(jnp.float32)
            date_term = jnp.dot(errors.T, group_bf, preferred_element_type=jnp.float32)
            return row_sum + row_term, date_term

        row_sum, date_terms = lax.scan(per_device, jnp.zeros((GROUP_ROWS, RANK), jnp.float32),
                                       (dates_bf, id_row, count_row, value_row, weight_row))
        return date_sum + date_terms, row_sum

    date_sum, row_sums = lax.scan(per_group, jnp.zeros((N_DATE, DATE_DEV, RANK), jnp.float32),
                                  (groups_bf, block_ids, block_counts, block_values, block_weights))
    pixel_next = (1.0 - DECAY) * pixel_now - (STEP_SCALE / DATES) * row_sums.reshape(PIXELS, RANK)
    dates_next = (1.0 - DECAY) * dates_now - (STEP_SCALE / PIXELS) * date_sum.reshape(DATES, RANK)
    return pixel_next, dates_next


def reference(pixel_factors, date_factors, block_ids, block_counts, block_values, block_weights):
    pixel_now = pixel_factors
    dates_now = date_factors
    for iteration in range(STEPS):
        pixel_now, dates_now = one_step(pixel_now, dates_now, block_ids, block_counts, block_values, block_weights)
    return pixel_now, dates_now
```

```python
import functools

import jax
import jax.numpy as jnp
from jax import lax
from jax.experimental import pallas as pl
from jax.experimental.pallas import tpu as pltpu
from jax.sharding import PartitionSpec as P

STEPS = 2
DECAY = 0.05
STEP_SCALE = 48.0
BLOCK_ROWS = 128
BLOCK_DATES = 64
LANES = 128
GROUP = 16
F32 = jnp.float32
BF16 = jnp.bfloat16
VMEM = pl.BlockSpec(memory_space=pltpu.VMEM)
SMEM = pl.BlockSpec(memory_space=pltpu.SMEM)


def params(mib):
    return pltpu.CompilerParams(vmem_limit_bytes=mib << 20)


def cost(flops, bytes_accessed):
    return pl.CostEstimate(flops=flops, bytes_accessed=bytes_accessed, transcendentals=0)


def row_pieces(rows):
    half = BLOCK_ROWS // 2
    for block in range(rows // BLOCK_ROWS):
        for odd in range(2):
            yield block * BLOCK_ROWS + odd * half, pl.ds(block * BLOCK_ROWS + odd, half, stride=2), half


def prepare_kernel(pixel_ref, date_ref, pixel_now_ref, pixel_bf_ref, date_bf_ref, slab):
    rows, rank = pixel_ref.shape
    for lane in range(0, rank, LANES):
        slab[lane // LANES] = pixel_ref[:, lane : lane + LANES]
    for to, source, half in row_pieces(rows):
        for lane in range(0, rank, LANES):
            piece = slab[lane // LANES, source, :]
            pixel_now_ref[to : to + half, lane : lane + LANES] = piece
            pixel_bf_ref[to : to + half, lane : lane + LANES] = piece.astype(BF16)
    date_bf_ref[...] = date_ref[...].astype(BF16)


def place_kernel(chip_blocks, place_ref, count_ref, ids_ref, values_ref, weights_ref, mine_ref, other_ref, flat):
    tiles = values_ref.shape[1] // LANES
    core_blocks = chip_blocks // 2
    chip, core = place_ref[0], place_ref[1]
    mine_ref[...] = jnp.zeros_like(mine_ref)
    other_ref[...] = jnp.zeros_like(other_ref)
    count = count_ref[0, 0]

    def group(g, carry):
        first = pl.multiple_of(g * GROUP, GROUP)
        for which, ref in enumerate((values_ref, weights_ref)):
            for t in range(tiles):
                flat[which, t * GROUP : (t + 1) * GROUP, :] = ref[
                    pl.ds(first, GROUP), t * LANES : (t + 1) * LANES
                ].astype(F32)
        for s in range(GROUP):
            row_block, date_block = ids_ref[0, first + s], ids_ref[1, first + s]
            target = lax.bitwise_xor(lax.div(row_block, chip_blocks), chip)
            inside = lax.rem(row_block, chip_blocks)
            parity = lax.div(inside, core_blocks)
            row = pl.multiple_of((target * core_blocks + lax.rem(inside, core_blocks)) * tiles, tiles)
            lane = pl.multiple_of(date_block * LANES, LANES)
            listed = first + s < count

            def put(ref, s=s, row=row, lane=lane):
                for which in range(2):
                    tile = flat[which, pl.ds(s, tiles, stride=GROUP), :]
                    ref[which, pl.ds(row, tiles), pl.ds(lane, LANES)] = tile.astype(BF16)

            pl.when(jnp.logical_and(listed, parity == core))(functools.partial(put, mine_ref))
            pl.when(jnp.logical_and(listed, parity != core))(functools.partial(put, other_ref))
        return carry

    lax.fori_loop(0, lax.div(count + GROUP - 1, GROUP), group, 0)


def apart(ref, which, first, rows):
    low = lax.broadcasted_iota(jnp.int32, (rows, LANES), 1) < BLOCK_DATES
    even, odd = [], []
    for pair in range(ref.shape[2] // (2 * LANES)):
        a = ref[which, first : first + rows, 2 * pair * LANES : (2 * pair + 1) * LANES].astype(F32)
        b = ref[which, first : first + rows, (2 * pair + 1) * LANES : (2 * pair + 2) * LANES].astype(F32)
        even.append(jnp.where(low, a, pltpu.roll(b, BLOCK_DATES, 1)))
        odd.append(jnp.where(low, pltpu.roll(a, BLOCK_DATES, 1), b))
    return jnp.concatenate([jnp.concatenate(even, axis=1), jnp.concatenate(odd, axis=1)], axis=0)


def chunk_kernel(n_recv, pixel_ref, dates_ref, dates_other_ref, mine_ref, other_ref, *rest):
    recv_refs, (term_ref, errors_ref) = rest[:n_recv], rest[n_recv:]
    half = BLOCK_ROWS // 2
    local = dates_ref.shape[0]
    for block in range(pixel_ref.shape[0] // BLOCK_ROWS):
        rows = slice(block * BLOCK_ROWS, (block + 1) * BLOCK_ROWS)
        total = None
        for k, (panel, dates) in enumerate(((mine_ref, dates_ref), (other_ref, dates_other_ref))):
            predicted = lax.dot_general(
                pixel_ref[rows, :], dates[...], (((1,), (1,)), ((), ())), preferred_element_type=F32
            )
            observed = apart(panel, 0, block * half, half)
            weights = apart(panel, 1, block * half, half)
            errors = (weights * (predicted - observed)).astype(BF16)
            errors_ref[rows, k * local : (k + 1) * local] = errors
            term = jnp.dot(errors, dates[...], preferred_element_type=F32)
            total = term if total is None else total + term
        for ref in recv_refs:
            total = total + ref[rows, :].astype(F32)
        term_ref[rows, :] = total.astype(term_ref.dtype)


def chunk(index, pixel_bf, dates_bf, dates_other, mine, other, recv, kind):
    rows, rank = pixel_bf.shape
    local = dates_bf.shape[0]
    panel = pl.BlockSpec((2, rows // 2, mine.shape[2]), lambda i: (0, index, 0))
    whole = lambda a: pl.BlockSpec(a.shape, lambda i: (0,) * a.ndim)
    return pl.pallas_call(
        functools.partial(chunk_kernel, len(recv)),
        grid=(1,),
        out_shape=(
            jax.ShapeDtypeStruct((rows, rank), kind),
            jax.ShapeDtypeStruct((rows, 2 * local), BF16),
        ),
        in_specs=[whole(pixel_bf), whole(dates_bf), whole(dates_other), panel, panel] + [whole(r) for r in recv],
        out_specs=(pl.BlockSpec((rows, rank), lambda i: (0, 0)), pl.BlockSpec((rows, 2 * local), lambda i: (0, 0))),
        compiler_params=params(24),
        cost_estimate=cost(8 * rows * rank * local, 1200000),
    )(pixel_bf, dates_bf, dates_other, mine, other, *recv)


def date_kernel(n, *refs):
    errors_refs, pixel_refs, (own_ref, other_ref) = refs[:n], refs[n : 2 * n], refs[2 * n :]
    local = own_ref.shape[0]
    for k, out in enumerate((own_ref, other_ref)):
        total = None
        for errors, pixels in zip(errors_refs, pixel_refs):
            term = lax.dot_general(
                errors[:, k * local : (k + 1) * local], pixels[...],
                (((0,), (0,)), ((), ())), preferred_element_type=F32,
            )
            total = term if total is None else total + term
        out[...] = total.astype(out.dtype)


def date_gradient(errors, pixels, local):
    rank = pixels[0].shape[1]
    n = len(errors)
    return pl.pallas_call(
        functools.partial(date_kernel, n),
        out_shape=(jax.ShapeDtypeStruct((local, rank), F32), jax.ShapeDtypeStruct((local, rank), BF16)),
        in_specs=[VMEM] * (2 * n),
        out_specs=(VMEM, VMEM),
        compiler_params=params(32),
        cost_estimate=cost(4 * n * pixels[0].shape[0] * rank * local, n * 400000),
    )(*errors, *pixels)


def pixel_kernel(scale, last, now_ref, *rest):
    parts, outs = rest[:-2], rest[-2:]
    rows, rank = now_ref.shape
    for start, target, half in row_pieces(rows):
        for lane in range(0, rank, LANES):
            at = (slice(start, start + half), slice(lane, lane + LANES))
            grad = parts[0][at].astype(F32)
            for part in parts[1:]:
                grad = grad + part[at].astype(F32)
            new = (1.0 - DECAY) * now_ref[at] - scale * grad
            if last:
                outs[1][lane // LANES, target, :] = new
            else:
                outs[0][at] = new
                outs[1][at] = new.astype(BF16)
    if last:
        for lane in range(0, rank, LANES):
            outs[0][:, lane : lane + LANES] = outs[1][lane // LANES]


def pixel_update(scale, last, now, parts):
    full = jax.ShapeDtypeStruct(now.shape, F32)
    return pl.pallas_call(
        functools.partial(pixel_kernel, scale, last),
        out_shape=(full,) if last else (full, jax.ShapeDtypeStruct(now.shape, BF16)),
        in_specs=[VMEM] * (1 + len(parts)),
        out_specs=(VMEM,) if last else (VMEM, VMEM),
        scratch_shapes=[pltpu.VMEM((now.shape[1] // LANES, now.shape[0], LANES), F32)] if last else [],
        compiler_params=params(16),
        cost_estimate=cost(10 * now.size, 8 * now.size),
    )(now, *parts)


def shards(pixel_factors, date_factors, block_ids, block_counts, block_values, block_weights):
    loop_size, groups = lax.axis_size("date"), lax.axis_size("pix")
    own_rows, rank = pixel_factors.shape
    local = date_factors.shape[0]
    chips = loop_size // 2
    high = min(4, chips)
    low = chips // high
    all_pixels = own_rows * loop_size * groups
    all_dates = local * loop_size
    slots, flat = block_values.shape[2:]
    me = lax.axis_index("date")
    tiles = flat // LANES
    core_blocks = own_rows // BLOCK_ROWS

    def swap(x, mask, axis="date"):
        return lax.ppermute(x, axis, [(i, i ^ mask) for i in range(lax.axis_size(axis))])

    shape = jax.ShapeDtypeStruct
    pixel_now, pixel_bf, dates_bf = pl.pallas_call(
        prepare_kernel,
        out_shape=(shape((own_rows, rank), F32), shape((own_rows, rank), BF16), shape((local, rank), BF16)),
        in_specs=[VMEM, VMEM],
        out_specs=(VMEM, VMEM, VMEM),
        scratch_shapes=[pltpu.VMEM((rank // LANES, own_rows, LANES), F32)],
        compiler_params=params(16),
        cost_estimate=cost(own_rows * rank, own_rows * rank * 16),
    )(pixel_factors, date_factors)
    dates_now = date_factors
    dates_other = swap(dates_bf, 1)

    panel = shape((2, chips * core_blocks * tiles, (local // BLOCK_DATES) * LANES), BF16)
    mine, other = pl.pallas_call(
        functools.partial(place_kernel, 2 * core_blocks),
        out_shape=(panel, panel),
        in_specs=[SMEM, SMEM, SMEM, VMEM, VMEM],
        out_specs=(VMEM, VMEM),
        scratch_shapes=[pltpu.VMEM((2, tiles * GROUP, LANES), F32)],
        compiler_params=params(32),
        cost_estimate=cost(slots * flat * 8, slots * flat * 8),
    )(
        jnp.stack([me // 2, me % 2]).astype(jnp.int32),
        block_counts,
        block_ids.reshape(2, slots),
        block_values.reshape(slots, flat),
        block_weights.reshape(slots, flat),
    )
    other = swap(other, 1)

    order = list(range(high - 1, -1, -1))
    for step in range(STEPS):
        last = step == STEPS - 1
        pixels = {}
        for hi in order:
            pixels[hi, 0] = swap(pixel_bf, 2 * low * hi) if hi else pixel_bf
        for hi in order:
            for lo in range(1, low):
                pixels[hi, lo] = swap(pixels[hi, 0], 2 * lo)
        errors, parts = {}, []
        for hi in order:
            recv = []
            for lo in range(1, low):
                term, errors[hi, lo] = chunk(
                    hi * low + lo, pixels[hi, lo], dates_bf, dates_other, mine, other, [], BF16
                )
                recv.append(swap(term, 2 * lo))
            term, errors[hi, 0] = chunk(
                hi * low, pixels[hi, 0], dates_bf, dates_other, mine, other, recv, BF16 if hi else F32
            )
            parts.append(swap(term, 2 * low * hi) if hi else term)
        keys = list(errors)
        own, partner = date_gradient([errors[k] for k in keys], [pixels[k] for k in keys], local)
        total = own + swap(partner, 1).astype(F32)
        mask = 1
        while mask < groups:
            rounded = total.astype(BF16)
            total = rounded.astype(F32) + swap(rounded, mask, "pix").astype(F32)
            mask *= 2
        dates_now = (1.0 - DECAY) * dates_now - STEP_SCALE / all_pixels * total
        if not last:
            dates_bf = dates_now.astype(BF16)
            dates_other = swap(dates_bf, 1)
            pixel_now, pixel_bf = pixel_update(STEP_SCALE / all_dates, False, pixel_now, parts)
        else:
            (pixel_now,) = pixel_update(STEP_SCALE / all_dates, True, pixel_now, parts)
    return (pixel_now, dates_now)


def solution(mesh):
    placed = (
        P(("pix", "date"), None),
        P("date", None),
        P("pix", "date", None, None),
        P("pix", "date"),
        P("pix", "date", None, None),
        P("pix", "date", None, None),
    )
    return jax.shard_map(
        shards,
        mesh=mesh,
        in_specs=placed,
        out_specs=(P(("pix", "date"), None), P("date", None)),
        check_vma=False,
    )
```

```python
import functools

import jax
import jax.numpy as jnp
from jax import lax
from jax.experimental import pallas as pl
from jax.experimental.pallas import tpu as pltpu
from jax.sharding import PartitionSpec as P

STEPS = 2
DECAY = 0.05
STEP_SCALE = 48.0
BLOCK_ROWS = 128
BLOCK_DATES = 64
LANES = 128
GROUP = 16
F32 = jnp.float32
BF16 = jnp.bfloat16
VMEM = pl.BlockSpec(memory_space=pltpu.VMEM)
HBM = pl.BlockSpec(memory_space=pltpu.HBM)
ANY = pl.BlockSpec(memory_space=pl.ANY)
SMEM = pl.BlockSpec(memory_space=pltpu.SMEM)


def params(mib):
    return pltpu.CompilerParams(vmem_limit_bytes=mib << 20)


def cost(flops, bytes_accessed):
    return pl.CostEstimate(flops=flops, bytes_accessed=bytes_accessed, transcendentals=0)


def row_pieces(rows):
    half = BLOCK_ROWS // 2
    for block in range(rows // BLOCK_ROWS):
        for odd in range(2):
            yield block * BLOCK_ROWS + odd * half, pl.ds(block * BLOCK_ROWS + odd, half, stride=2), half


def prepare_kernel(pixel_ref, date_ref, pixel_now_ref, pixel_bf_ref, date_bf_ref, slab):
    rows, rank = pixel_ref.shape
    for lane in range(0, rank, LANES):
        slab[lane // LANES] = pixel_ref[:, lane : lane + LANES]
    for to, source, half in row_pieces(rows):
        for lane in range(0, rank, LANES):
            piece = slab[lane // LANES, source, :]
            pixel_now_ref[to : to + half, lane : lane + LANES] = piece
            pixel_bf_ref[to : to + half, lane : lane + LANES] = piece.astype(BF16)
    date_bf_ref[...] = date_ref[...].astype(BF16)


def place_kernel(chip_blocks, place_ref, *refs):
    ids_refs, count_refs, block_refs = refs[0:2], refs[2:4], (refs[4:6], refs[6:8])
    panel_ref, raw, flat, sems = refs[-4:]
    slots, size = block_refs[0][0].shape
    tiles = size // LANES
    core_blocks = chip_blocks // 2
    chip, core = place_ref[0], place_ref[1]
    spare = panel_ref.shape[1] - tiles
    width = panel_ref.shape[2] // 2

    def load(k, g, which):
        rows = pl.ds(pl.multiple_of(g * GROUP, GROUP), GROUP)
        return pltpu.make_async_copy(block_refs[k][which].at[rows], raw.at[k, which, rows], sems.at[k, which, g])

    for k in range(2):
        for g in range(slots // GROUP):
            for which in range(2):
                load(k, g, which).start()
    panel_ref[...] = jnp.zeros_like(panel_ref)

    for k in range(2):
        count = count_refs[k][0, 0]

        def group(g, carry, k=k, count=count):
            first = pl.multiple_of(g * GROUP, GROUP)
            for which in range(2):
                load(k, g, which).wait()

            @pl.when(first < count)
            def _():
                for which in range(2):
                    for t in range(tiles):
                        flat[which, t * GROUP : (t + 1) * GROUP, :] = raw[
                            k, which, pl.ds(first, GROUP), t * LANES : (t + 1) * LANES
                        ].astype(F32)
                for s in range(GROUP):
                    row_block, date_block = ids_refs[k][0, first + s], ids_refs[k][1, first + s]
                    target = lax.bitwise_xor(lax.div(row_block, chip_blocks), chip)
                    inside = lax.rem(row_block, chip_blocks)
                    wanted = jnp.logical_and(lax.div(inside, core_blocks) == core, first + s < count)
                    row = (target * core_blocks + lax.rem(inside, core_blocks)) * tiles
                    row = pl.multiple_of(jnp.where(wanted, row, spare), tiles)
                    lane = pl.multiple_of(k * width + date_block * LANES, LANES)
                    for which in range(2):
                        tile = flat[which, pl.ds(s, tiles, stride=GROUP), :]
                        panel_ref[which, pl.ds(row, tiles), pl.ds(lane, LANES)] = tile.astype(BF16)

            return carry

        lax.fori_loop(0, slots // GROUP, group, 0)


def apart(ref, which, first, rows, lane, width):
    low = lax.broadcasted_iota(jnp.int32, (rows, LANES), 1) < BLOCK_DATES
    even, odd = [], []
    for at in range(lane, lane + width, 2 * LANES):
        a = ref[which, first : first + rows, at : at + LANES].astype(F32)
        b = ref[which, first : first + rows, at + LANES : at + 2 * LANES].astype(F32)
        even.append(jnp.where(low, a, pltpu.roll(b, BLOCK_DATES, 1)))
        odd.append(jnp.where(low, pltpu.roll(a, BLOCK_DATES, 1), b))
    return jnp.concatenate([jnp.concatenate(even, axis=1), jnp.concatenate(odd, axis=1)], axis=0)


def chunk_kernel(n, n_recv, n_after, *refs):
    pixel_refs, (dates_ref, dates_other_ref, panel_ref) = refs[:n], refs[n : n + 3]
    recv_refs, (term_ref, errors_ref) = refs[n + 3 : n + 3 + n_recv], refs[-2:]
    width = panel_ref.shape[2] // 2
    half = BLOCK_ROWS // 2
    local = dates_ref.shape[0]
    blocks = pixel_refs[0].shape[0] // BLOCK_ROWS
    for block in range(n * blocks):
        inside = slice(block % blocks * BLOCK_ROWS, (block % blocks + 1) * BLOCK_ROWS)
        rows = slice(block * BLOCK_ROWS, (block + 1) * BLOCK_ROWS)
        total = None
        for k, dates in enumerate((dates_ref, dates_other_ref)):
            predicted = lax.dot_general(
                pixel_refs[block // blocks][inside, :], dates[...],
                (((1,), (1,)), ((), ())), preferred_element_type=F32,
            )
            observed = apart(panel_ref, 0, block * half, half, k * width, width)
            weights = apart(panel_ref, 1, block * half, half, k * width, width)
            errors = (weights * (predicted - observed)).astype(BF16)
            errors_ref[rows, k * local : (k + 1) * local] = errors
            term = jnp.dot(errors, dates[...], preferred_element_type=F32)
            total = term if total is None else total + term
        for ref in recv_refs:
            total = total + ref[rows, :].astype(F32)
        term_ref[rows, :] = total.astype(term_ref.dtype)


def chunk(pixels, dates_bf, dates_other, panel, at, recv, kind, after):
    rows, rank = pixels[0].shape
    local = dates_bf.shape[0]
    n = len(pixels)
    whole = lambda a: pl.BlockSpec(a.shape, lambda i: (0,) * a.ndim)
    block = lambda at: pl.BlockSpec((rows, rank), lambda i: (at, 0))
    return pl.pallas_call(
        functools.partial(chunk_kernel, n, len(recv), len(after)),
        grid=(1,),
        out_shape=(
            jax.ShapeDtypeStruct((n * rows, rank), kind),
            jax.ShapeDtypeStruct((n * rows, 2 * local), BF16),
        ),
        in_specs=[whole(p) for p in pixels] + [whole(dates_bf), whole(dates_other), pl.BlockSpec((2, n * rows // 2, panel.shape[2]), lambda i: (0, at, 0))]
        + [block(at) for _, at in recv] + [ANY] * len(after),
        out_specs=(block(0) if n == 1 else pl.BlockSpec((n * rows, rank), lambda i: (0, 0)),
                   pl.BlockSpec((n * rows, 2 * local), lambda i: (0, 0))),
        compiler_params=params(24),
        cost_estimate=cost(8 * n * rows * rank * local, n * 1200000),
    )(*pixels, dates_bf, dates_other, panel, *[r for r, _ in recv], *after)


def hold_kernel(x_ref, after_ref, out_ref):
    out_ref[...] = x_ref[...]


def hold(x, after):
    return pl.pallas_call(
        hold_kernel,
        out_shape=jax.ShapeDtypeStruct(x.shape, x.dtype),
        in_specs=[VMEM, ANY],
        out_specs=VMEM,
        compiler_params=params(16),
        cost_estimate=cost(x.size, 4 * x.size),
    )(x, after)


def date_kernel(starts, *refs):
    n = len(starts)
    pixel_refs, errors_refs, (own_ref, other_ref) = refs[:n], refs[n:-2], refs[-2:]
    local = own_ref.shape[0]
    for k, out in enumerate((own_ref, other_ref)):
        total = None
        for (which, start), pixels in zip(starts, pixel_refs):
            errors = errors_refs[which][start : start + pixels.shape[0], k * local : (k + 1) * local]
            term = lax.dot_general(errors, pixels[...], (((0,), (0,)), ((), ())), preferred_element_type=F32)
            total = term if total is None else total + term
        out[...] = total.astype(out.dtype)


def date_gradient(errors, pixels, starts, local, after):
    rank = pixels[0].shape[1]
    n = len(pixels)
    return pl.pallas_call(
        functools.partial(date_kernel, starts),
        out_shape=(jax.ShapeDtypeStruct((local, rank), BF16),) * 2,
        in_specs=[VMEM] * (n + len(errors)) + [ANY] * len(after),
        out_specs=(VMEM, VMEM),
        compiler_params=params(32),
        cost_estimate=cost(4 * n * pixels[0].shape[0] * rank * local, n * 400000),
    )(*pixels, *errors, *after)


def sum_kernel(*refs):
    parts, out_ref = refs[:-1], refs[-1]
    total = parts[0][...].astype(F32)
    for part in parts[1:]:
        total = total + part[...].astype(F32)
    out_ref[...] = total


def pixel_kernel(scale, last, now_ref, *rest):
    parts, outs = rest[:-2], rest[-2:]
    rows, rank = now_ref.shape
    for start, target, half in row_pieces(rows):
        for lane in range(0, rank, LANES):
            at = (slice(start, start + half), slice(lane, lane + LANES))
            grad = parts[0][at].astype(F32)
            for part in parts[1:]:
                grad = grad + part[at].astype(F32)
            new = (1.0 - DECAY) * now_ref[at] - scale * grad
            if last:
                outs[1][lane // LANES, target, :] = new
            else:
                outs[0][at] = new
                outs[1][at] = new.astype(BF16)
    if last:
        for lane in range(0, rank, LANES):
            outs[0][:, lane : lane + LANES] = outs[1][lane // LANES]


def pixel_update(scale, last, now, parts):
    full = jax.ShapeDtypeStruct(now.shape, F32)
    first = pl.BlockSpec(now.shape, lambda i: (0, 0))
    early = pl.pallas_call(
        sum_kernel,
        grid=(1,),
        out_shape=full,
        in_specs=[first] * (len(parts) - 1),
        out_specs=first,
        compiler_params=params(16),
        cost_estimate=cost(4 * now.size, 8 * now.size),
    )(*parts[:-1])
    return pl.pallas_call(
        functools.partial(pixel_kernel, scale, last),
        out_shape=(full,) if last else (full, jax.ShapeDtypeStruct(now.shape, BF16)),
        in_specs=[VMEM] * 3,
        out_specs=(VMEM,) if last else (VMEM, VMEM),
        scratch_shapes=[pltpu.VMEM((now.shape[1] // LANES, now.shape[0], LANES), F32)] if last else [],
        compiler_params=params(16),
        cost_estimate=cost(10 * now.size, 8 * now.size),
    )(now, early, parts[-1])


def date_update_kernel(scale, now_ref, *refs):
    parts, (after_ref, new_ref, bf_ref) = refs[:-3], refs[-3:]
    halves = [None, None]
    for i, part in enumerate(parts):
        side = 2 * i // len(parts)
        value = part[...].astype(F32)
        halves[side] = value if halves[side] is None else halves[side] + value
    new = (1.0 - DECAY) * now_ref[...] - scale * (halves[0] + halves[1])
    new_ref[...] = new
    bf_ref[...] = new.astype(BF16)


def date_update(scale, now, parts, after):
    return pl.pallas_call(
        functools.partial(date_update_kernel, scale),
        out_shape=(jax.ShapeDtypeStruct(now.shape, F32), jax.ShapeDtypeStruct(now.shape, BF16)),
        in_specs=[VMEM] * (1 + len(parts)) + [ANY],
        out_specs=(VMEM, VMEM),
        compiler_params=params(16),
        cost_estimate=cost(8 * now.size, 8 * now.size),
    )(now, *parts, after)


def shards(pixel_factors, date_factors, block_ids, block_counts, block_values, block_weights):
    loop_size, groups = lax.axis_size("date"), lax.axis_size("pix")
    own_rows, rank = pixel_factors.shape
    local = date_factors.shape[0]
    chips = loop_size // 2
    high = 4
    low = chips // high
    all_pixels = own_rows * loop_size * groups
    all_dates = local * loop_size
    slots, flat = block_values.shape[2:]
    me = lax.axis_index("date")
    tiles = flat // LANES
    core_blocks = own_rows // BLOCK_ROWS

    def swap(x, mask, axis="date"):
        return lax.ppermute(x, axis, [(i, i ^ mask) for i in range(lax.axis_size(axis))])

    shape = jax.ShapeDtypeStruct
    pixel_now, pixel_bf, dates_bf = pl.pallas_call(
        prepare_kernel,
        out_shape=(shape((own_rows, rank), F32), shape((own_rows, rank), BF16), shape((local, rank), BF16)),
        in_specs=[VMEM, VMEM],
        out_specs=(VMEM, VMEM, VMEM),
        scratch_shapes=[pltpu.VMEM((rank // LANES, own_rows, LANES), F32)],
        compiler_params=params(16),
        cost_estimate=cost(own_rows * rank, own_rows * rank * 16),
    )(pixel_factors, date_factors)
    dates_now = date_factors
    dates_other = swap(dates_bf, 1)

    rows, width = chips * core_blocks * tiles, local // BLOCK_DATES * LANES
    ids, values, weights = (
        block_ids.reshape(2, slots), block_values.reshape(slots, flat), block_weights.reshape(slots, flat)
    )
    panel = pl.pallas_call(
        functools.partial(place_kernel, 2 * core_blocks),
        out_shape=shape((2, rows + tiles, 2 * width), BF16),
        in_specs=[SMEM] * 5 + [HBM] * 4,
        out_specs=VMEM,
        scratch_shapes=[
            pltpu.VMEM((2, 2, slots, flat), BF16),
            pltpu.VMEM((2, tiles * GROUP, LANES), F32),
            pltpu.SemaphoreType.DMA((2, 2, slots // GROUP)),
        ],
        compiler_params=params(36),
        cost_estimate=cost(slots * flat * 8, slots * flat * 8),
    )(
        jnp.stack([me // 2, me % 2]).astype(jnp.int32),
        ids, swap(ids, 1), block_counts, swap(block_counts, 1),
        values, weights, swap(values, 1), swap(weights, 1),
    )

    for step in range(STEPS):
        last = step == STEPS - 1
        far = range(1, low)
        along = [2 * low * hi for hi in range(high)]
        pixels = {(0, 0): pixel_bf}
        pixels[3, 0] = swap(pixel_bf, along[3])
        for lo in far:
            pixels[0, lo] = swap(pixel_bf, 2 * lo)
        pixels[1, 0] = swap(pixel_bf, along[1])
        pixels[2, 0] = swap(hold(pixel_bf, pixels[0, 1]), along[2])
        for lo in far:
            pixels[1, lo] = swap(pixels[1, 0], 2 * lo)
            pixels[3, lo] = swap(pixels[3, 0], 2 * lo)
            pixels[2, lo] = swap(pixels[2, 0], 2 * lo)
        errors, starts, ordered, after = [], [], [], []

        def terms(keys, recv, kind, errors=errors, starts=starts, ordered=ordered, dates_bf=dates_bf,
                  dates_other=dates_other, pixels=pixels):
            nonlocal after
            hi, lo = keys[0]
            n = len(keys)
            term, error = chunk(
                [pixels[k] for k in keys], dates_bf, dates_other, panel, (hi * low + lo) // n, recv, kind, after,
            )
            starts += [(len(errors), i * own_rows) for i in range(n)]
            errors.append(error)
            ordered += [pixels[k] for k in keys]
            after = [term]
            return term

        pair = swap(terms([(1, lo) for lo in range(low)], [], BF16), along[1])
        parts = [terms([(0, 0)], [], F32), pair]
        recv3 = [swap(terms([(3, lo)], [], BF16), 2 * lo) for lo in far]
        recv2 = [swap(terms([(2, lo)], [], BF16), 2 * lo) for lo in far]
        part3 = swap(terms([(3, 0)], [(r, 0) for r in recv3], BF16), along[3])
        parts += [swap(terms([(0, lo)], [(pair, lo)], BF16), 2 * lo) for lo in far]
        parts += [part3, swap(terms([(2, 0)], [(r, 0) for r in recv2], BF16), along[2])]
        own, partner = date_gradient(errors, ordered, tuple(starts), local, [])
        scale = STEP_SCALE / all_dates
        if last:
            (pixel_now,) = pixel_update(scale, True, pixel_now, parts)
        else:
            pixel_now, pixel_bf = pixel_update(scale, False, pixel_now, parts)
        sums = [own, swap(partner, 1)]
        if groups > 1:
            count = groups * loop_size
            across = [(i, i ^ (loop_size + 1)) for i in range(count)]
            sums += [swap(own, 1, "pix"), lax.ppermute(partner, ("pix", "date"), across)]
        mask = 2
        while mask < groups:
            left, right = sums[: len(sums) // 2], sums[len(sums) // 2 :]
            total = sum(x.astype(F32) for x in left) + sum(x.astype(F32) for x in right)
            sums = [total.astype(BF16)]
            sums.append(swap(sums[0], mask, "pix"))
            mask *= 2
        dates_now, dates_bf = date_update(
            STEP_SCALE / all_pixels, dates_now, sums, pixel_now if last else pixel_bf
        )
        if not last:
            dates_other = swap(dates_bf, 1)
    return (pixel_now, dates_now)


def solution(mesh):
    placed = (
        P(("pix", "date"), None),
        P("date", None),
        P("pix", "date", None, None),
        P("pix", "date"),
        P("pix", "date", None, None),
        P("pix", "date", None, None),
    )
    return jax.shard_map(
        shards,
        mesh=mesh,
        in_specs=placed,
        out_specs=(P(("pix", "date"), None), P("date", None)),
        check_vma=False,
    )
```

```python
import functools

import jax
import jax.numpy as jnp
from jax import lax
from jax.experimental import pallas as pl
from jax.experimental.pallas import tpu as pltpu
from jax.sharding import PartitionSpec as P

STEPS = 2
DECAY = 0.05
STEP_SCALE = 48.0
BLOCK_ROWS = 128
BLOCK_DATES = 64
LANES = 128
GROUP = 16
F32 = jnp.float32
BF16 = jnp.bfloat16
VMEM = pl.BlockSpec(memory_space=pltpu.VMEM)
HBM = pl.BlockSpec(memory_space=pltpu.HBM)
ANY = pl.BlockSpec(memory_space=pl.ANY)
SMEM = pl.BlockSpec(memory_space=pltpu.SMEM)


def params(mib):
    return pltpu.CompilerParams(vmem_limit_bytes=mib << 20)


def cost(flops, bytes_accessed):
    return pl.CostEstimate(flops=flops, bytes_accessed=bytes_accessed, transcendentals=0)


def row_pieces(rows):
    half = BLOCK_ROWS // 2
    for block in range(rows // BLOCK_ROWS):
        for odd in range(2):
            yield block * BLOCK_ROWS + odd * half, pl.ds(block * BLOCK_ROWS + odd, half, stride=2), half


def prepare_kernel(pixel_ref, pixel_now_ref, pixel_bf_ref, slab):
    rows, rank = pixel_ref.shape
    for lane in range(0, rank, LANES):
        slab[lane // LANES] = pixel_ref[:, lane : lane + LANES]
    for to, source, half in row_pieces(rows):
        for lane in range(0, rank, LANES):
            piece = slab[lane // LANES, source, :]
            pixel_now_ref[to : to + half, lane : lane + LANES] = piece
            pixel_bf_ref[to : to + half, lane : lane + LANES] = piece.astype(BF16)


def place_kernel(copies, chip_blocks, place_ref, ids_ref, values_ref, weights_ref, panel_ref, flat, *scratch):
    slots, size = values_ref.shape
    tiles = size // LANES
    core_blocks = chip_blocks // 2
    chip, core, count = place_ref[0], place_ref[1], ids_ref[2, 0]
    spare = panel_ref.shape[1] - tiles
    refs = (values_ref, weights_ref)

    def load(g, which):
        raw, sems = scratch
        rows = pl.ds(pl.multiple_of(g * GROUP, GROUP), GROUP)
        return pltpu.make_async_copy(refs[which].at[rows], raw.at[which, rows], sems.at[which, g])

    if copies:
        for g in range(slots // GROUP):
            for which in range(2):
                load(g, which).start()
    panel_ref[...] = jnp.zeros_like(panel_ref)

    def group(g, carry):
        first = pl.multiple_of(g * GROUP, GROUP)
        if copies:
            for which in range(2):
                load(g, which).wait()

        @pl.when(first < count)
        def _():
            for which in range(2):
                source = scratch[0].at[which] if copies else refs[which]
                for t in range(tiles):
                    flat[which, t * GROUP : (t + 1) * GROUP, :] = source[
                        pl.ds(first, GROUP), t * LANES : (t + 1) * LANES
                    ].astype(F32)
            for s in range(GROUP):
                row_block, date_block = ids_ref[0, first + s], ids_ref[1, first + s]
                target = lax.bitwise_xor(lax.div(row_block, chip_blocks), chip)
                inside = lax.rem(row_block, chip_blocks)
                wanted = jnp.logical_and(lax.div(inside, core_blocks) == core, first + s < count)
                row = (target * core_blocks + lax.rem(inside, core_blocks)) * tiles
                row = pl.multiple_of(jnp.where(wanted, row, spare), tiles)
                lane = pl.multiple_of(date_block * LANES, LANES)
                for which in range(2):
                    tile = flat[which, pl.ds(s, tiles, stride=GROUP), :]
                    panel_ref[which, pl.ds(row, tiles), pl.ds(lane, LANES)] = tile.astype(BF16)

        return carry

    lax.fori_loop(0, slots // GROUP, group, 0)


def place_blocks(copies, core_blocks, place, ids, values, weights, rows, width, mib):
    slots, size = values.shape
    tiles = size // LANES
    scratch = [pltpu.VMEM((2, slots, size), BF16), pltpu.SemaphoreType.DMA((2, slots // GROUP))] if copies else []
    return pl.pallas_call(
        functools.partial(place_kernel, copies, 2 * core_blocks),
        out_shape=jax.ShapeDtypeStruct((2, rows + tiles, width), BF16),
        in_specs=[SMEM, SMEM] + [HBM if copies else VMEM] * 2,
        out_specs=VMEM,
        scratch_shapes=[pltpu.VMEM((2, tiles * GROUP, LANES), F32)] + scratch,
        compiler_params=params(mib),
        cost_estimate=cost(slots * size * 8, slots * size * 8),
    )(place, ids, values, weights)


def pack_kernel(count_ref, date_ref, ids_ref, out_ref):
    local, rank = date_ref.shape
    slots = ids_ref.shape[1]
    out_ref[:local, :] = date_ref[...].astype(BF16)
    row = lax.broadcasted_iota(jnp.int32, (GROUP, slots), 0)
    ids = jnp.where(row == 0, ids_ref[0:1, :], jnp.where(row == 1, ids_ref[1:2, :], count_ref[0, 0]))
    out_ref[local:, :] = jnp.zeros((GROUP, rank), BF16)
    out_ref[local:, :slots] = ids.astype(F32).astype(BF16)


def apart(ref, which, first, rows):
    low = lax.broadcasted_iota(jnp.int32, (rows, LANES), 1) < BLOCK_DATES
    even, odd = [], []
    for at in range(0, ref.shape[2], 2 * LANES):
        a = ref[which, first : first + rows, at : at + LANES].astype(F32)
        b = ref[which, first : first + rows, at + LANES : at + 2 * LANES].astype(F32)
        even.append(jnp.where(low, a, pltpu.roll(b, BLOCK_DATES, 1)))
        odd.append(jnp.where(low, pltpu.roll(a, BLOCK_DATES, 1), b))
    return jnp.concatenate([jnp.concatenate(even, axis=1), jnp.concatenate(odd, axis=1)], axis=0)


def chunk_kernel(n, *refs):
    pixel_refs, (dates_ref, dates_other_ref, mine_ref, other_ref) = refs[:n], refs[n : n + 4]
    term_ref, errors_ref = refs[-2:]
    half = BLOCK_ROWS // 2
    local = dates_ref.shape[0]
    blocks = pixel_refs[0].shape[0] // BLOCK_ROWS
    for block in range(n * blocks):
        inside = slice(block % blocks * BLOCK_ROWS, (block % blocks + 1) * BLOCK_ROWS)
        rows = slice(block * BLOCK_ROWS, (block + 1) * BLOCK_ROWS)
        total = None
        for k, (panel, dates) in enumerate(((mine_ref, dates_ref), (other_ref, dates_other_ref))):
            predicted = lax.dot_general(
                pixel_refs[block // blocks][inside, :], dates[...],
                (((1,), (1,)), ((), ())), preferred_element_type=F32,
            )
            observed = apart(panel, 0, block * half, half)
            weights = apart(panel, 1, block * half, half)
            errors = (weights * (predicted - observed)).astype(BF16)
            errors_ref[rows, k * local : (k + 1) * local] = errors
            term = jnp.dot(errors, dates[...], preferred_element_type=F32)
            total = term if total is None else total + term
        term_ref[rows, :] = total.astype(term_ref.dtype)


def chunk(pixels, dates_bf, dates_other, panels, at, kind, after):
    rows, rank = pixels[0].shape
    local = panels[0].shape[2] // 2
    n = len(pixels)
    whole = lambda a: pl.BlockSpec(a.shape, lambda i: (0,) * a.ndim)
    dates = pl.BlockSpec((local, rank), lambda i: (0, 0))
    panel = pl.BlockSpec((2, n * rows // 2, panels[0].shape[2]), lambda i: (0, at, 0))
    return pl.pallas_call(
        functools.partial(chunk_kernel, n),
        grid=(1,),
        out_shape=(
            jax.ShapeDtypeStruct((n * rows, rank), kind),
            jax.ShapeDtypeStruct((n * rows, 2 * local), BF16),
        ),
        in_specs=[whole(p) for p in pixels] + [dates, dates, panel, panel]
        + [ANY] * len(after),
        out_specs=(pl.BlockSpec((n * rows, rank), lambda i: (0, 0)),
                   pl.BlockSpec((n * rows, 2 * local), lambda i: (0, 0))),
        compiler_params=params(24),
        cost_estimate=cost(8 * n * rows * rank * local, n * 1200000),
    )(*pixels, dates_bf, dates_other, *panels, *after)


def hold_kernel(x_ref, *refs):
    refs[-1][...] = x_ref[...]


def hold(x, *after):
    return pl.pallas_call(
        hold_kernel,
        out_shape=jax.ShapeDtypeStruct(x.shape, x.dtype),
        in_specs=[VMEM] + [ANY] * len(after),
        out_specs=VMEM,
        compiler_params=params(16),
        cost_estimate=cost(x.size, 4 * x.size),
    )(x, *after)


def date_kernel(starts, *refs):
    n = len(starts)
    pixel_refs, errors_refs, (own_ref, other_ref) = refs[:n], refs[n:-2], refs[-2:]
    local = own_ref.shape[0]
    for k, out in enumerate((own_ref, other_ref)):
        total = None
        for (which, start), pixels in zip(starts, pixel_refs):
            errors = errors_refs[which][start : start + pixels.shape[0], k * local : (k + 1) * local]
            term = lax.dot_general(errors, pixels[...], (((0,), (0,)), ((), ())), preferred_element_type=F32)
            total = term if total is None else total + term
        out[...] = total.astype(out.dtype)


def date_gradient(errors, pixels, starts, local, after):
    rank = pixels[0].shape[1]
    n = len(pixels)
    return pl.pallas_call(
        functools.partial(date_kernel, starts),
        out_shape=(jax.ShapeDtypeStruct((local, rank), BF16),) * 2,
        in_specs=[VMEM] * (n + len(errors)) + [ANY] * len(after),
        out_specs=(VMEM, VMEM),
        compiler_params=params(32),
        cost_estimate=cost(4 * n * pixels[0].shape[0] * rank * local, n * 400000),
    )(*pixels, *errors, *after)


def sum_kernel(*refs):
    parts, out_ref = refs[:-1], refs[-1]
    total = parts[0][...].astype(F32)
    for part in parts[1:]:
        total = total + part[...].astype(F32)
    out_ref[...] = total.astype(out_ref.dtype)


def add(parts, kind):
    rows, rank = parts[0][0].shape
    block = lambda at: pl.BlockSpec((rows, rank), lambda i: (at, 0))
    return pl.pallas_call(
        sum_kernel,
        grid=(1,),
        out_shape=jax.ShapeDtypeStruct((rows, rank), kind),
        in_specs=[block(at) for _, at in parts],
        out_specs=block(0),
        compiler_params=params(16),
        cost_estimate=cost(4 * rows * rank, 8 * rows * rank),
    )(*[x for x, _ in parts])


def pixel_kernel(scale, last, now_ref, *rest):
    parts, outs = rest[:-2], rest[-2:]
    rows, rank = now_ref.shape
    for start, target, half in row_pieces(rows):
        for lane in range(0, rank, LANES):
            at = (slice(start, start + half), slice(lane, lane + LANES))
            grad = parts[0][at].astype(F32)
            for part in parts[1:]:
                grad = grad + part[at].astype(F32)
            new = (1.0 - DECAY) * now_ref[at] - scale * grad
            if last:
                outs[1][lane // LANES, target, :] = new
            else:
                outs[0][at] = new
                outs[1][at] = new.astype(BF16)
    if last:
        for lane in range(0, rank, LANES):
            outs[0][:, lane : lane + LANES] = outs[1][lane // LANES]


def pixel_update(scale, last, now, parts):
    full = jax.ShapeDtypeStruct(now.shape, F32)
    early = add([(part, 0) for part in parts[:-1]], F32)
    return pl.pallas_call(
        functools.partial(pixel_kernel, scale, last),
        out_shape=(full,) if last else (full, jax.ShapeDtypeStruct(now.shape, BF16)),
        in_specs=[VMEM] * 3,
        out_specs=(VMEM,) if last else (VMEM, VMEM),
        scratch_shapes=[pltpu.VMEM((now.shape[1] // LANES, now.shape[0], LANES), F32)] if last else [],
        compiler_params=params(16),
        cost_estimate=cost(10 * now.size, 8 * now.size),
    )(now, early, parts[-1])


def date_update_kernel(scale, now_ref, *refs):
    parts, (after_ref, new_ref, bf_ref) = refs[:-3], refs[-3:]
    halves = [None, None]
    for i, part in enumerate(parts):
        side = 2 * i // len(parts)
        value = part[...].astype(F32)
        halves[side] = value if halves[side] is None else halves[side] + value
    new = (1.0 - DECAY) * now_ref[...] - scale * (halves[0] + halves[1])
    new_ref[...] = new
    bf_ref[...] = new.astype(BF16)


def date_update(scale, now, parts, after):
    return pl.pallas_call(
        functools.partial(date_update_kernel, scale),
        out_shape=(jax.ShapeDtypeStruct(now.shape, F32), jax.ShapeDtypeStruct(now.shape, BF16)),
        in_specs=[VMEM] * (1 + len(parts)) + [ANY],
        out_specs=(VMEM, VMEM),
        compiler_params=params(16),
        cost_estimate=cost(8 * now.size, 8 * now.size),
    )(now, *parts, after)


def shards(pixel_factors, date_factors, block_ids, block_counts, block_values, block_weights):
    loop_size, groups = lax.axis_size("date"), lax.axis_size("pix")
    own_rows, rank = pixel_factors.shape
    local = date_factors.shape[0]
    chips = loop_size // 2
    high = 4
    low = chips // high
    all_pixels = own_rows * loop_size * groups
    all_dates = local * loop_size
    slots, flat = block_values.shape[2:]
    me = lax.axis_index("date")
    tiles = flat // LANES
    core_blocks = own_rows // BLOCK_ROWS

    def swap(x, mask, axis="date"):
        return lax.ppermute(x, axis, [(i, i ^ mask) for i in range(lax.axis_size(axis))])

    shape = jax.ShapeDtypeStruct
    pixel_now, pixel_bf = pl.pallas_call(
        prepare_kernel,
        out_shape=(shape((own_rows, rank), F32), shape((own_rows, rank), BF16)),
        in_specs=[VMEM],
        out_specs=(VMEM, VMEM),
        scratch_shapes=[pltpu.VMEM((rank // LANES, own_rows, LANES), F32)],
        compiler_params=params(16),
        cost_estimate=cost(own_rows * rank, own_rows * rank * 16),
    )(pixel_factors)
    dates_now = date_factors
    block_lists = block_ids.reshape(2, slots)
    dates_bf = pl.pallas_call(
        pack_kernel,
        out_shape=shape((local + GROUP, rank), BF16),
        in_specs=[SMEM, VMEM, VMEM],
        out_specs=VMEM,
        compiler_params=params(16),
        cost_estimate=cost(local * rank, 6 * local * rank),
    )(block_counts, date_factors, block_lists)
    dates_other = swap(dates_bf, 1)

    def lists(packed):
        return packed[local : local + 3, :slots].astype(jnp.int32)

    rows, width = chips * core_blocks * tiles, local // BLOCK_DATES * LANES
    values, weights = block_values.reshape(slots, flat), block_weights.reshape(slots, flat)
    place = jnp.stack([me // 2, me % 2]).astype(jnp.int32)
    mine = place_blocks(True, core_blocks, place, lists(dates_bf), values, weights, rows, width, 36)
    other = place_blocks(
        False, core_blocks, place, lists(dates_other), swap(values, 1), swap(weights, 1), rows, width, 30
    )
    panels = (mine, other)

    for step in range(STEPS):
        last = step == STEPS - 1
        far = range(1, low)
        along = [2 * low * hi for hi in range(high)]
        pixels = {(0, 0): pixel_bf}
        pixels[3, 0] = swap(pixel_bf, along[3])
        for lo in far:
            pixels[0, lo] = swap(pixel_bf, 2 * lo)
        pixels[1, 0] = swap(pixel_bf, along[1])
        pixels[2, 0] = swap(hold(pixel_bf, pixels[0, 1], *([] if step else [mine])), along[2])
        for lo in far:
            pixels[1, lo] = swap(pixels[1, 0], 2 * lo)
            pixels[3, lo] = swap(pixels[3, 0], 2 * lo)
            pixels[2, lo] = swap(pixels[2, 0] if step else hold(pixels[2, 0], other), 2 * lo)
        errors, starts, ordered, after = [], [], [], []

        def terms(keys, kind, errors=errors, starts=starts, ordered=ordered, dates_bf=dates_bf,
                  dates_other=dates_other, pixels=pixels):
            nonlocal after
            hi, lo = keys[0]
            n = len(keys)
            term, error = chunk(
                [pixels[k] for k in keys], dates_bf, dates_other, panels, (hi * low + lo) // n, kind, after,
            )
            starts += [(len(errors), i * own_rows) for i in range(n)]
            errors.append(error)
            ordered += [pixels[k] for k in keys]
            after = [term]
            return term

        pair = swap(terms([(1, lo) for lo in range(low)], BF16), along[1])
        recv3 = [(swap(terms([(3, lo)], BF16), 2 * lo), 0) for lo in far]
        near3 = terms([(3, 0)], F32)
        near2 = terms([(2, 0)], F32)
        near0 = terms([(0, 0)], F32)
        row0 = [terms([(0, lo)], F32) for lo in far]
        recv2 = [(swap(terms([(2, lo)], BF16), 2 * lo), 0) for lo in far]
        part3 = swap(add([(near3, 0)] + recv3, BF16), along[3])
        part0 = [swap(add([(row0[lo - 1], 0), (pair, lo)], BF16), 2 * lo) for lo in far]
        part2 = swap(add([(near2, 0)] + recv2, BF16), along[2])
        parts = [near0, pair] + part0 + [part3, part2]
        own, partner = date_gradient(errors, ordered, tuple(starts), local, [])
        scale = STEP_SCALE / all_dates
        if last:
            (pixel_now,) = pixel_update(scale, True, pixel_now, parts)
        else:
            pixel_now, pixel_bf = pixel_update(scale, False, pixel_now, parts)
        sums = [own, swap(partner, 1)]
        if groups > 1:
            count = groups * loop_size
            across = [(i, i ^ (loop_size + 1)) for i in range(count)]
            sums += [swap(own, 1, "pix"), lax.ppermute(partner, ("pix", "date"), across)]
        mask = 2
        while mask < groups:
            left, right = sums[: len(sums) // 2], sums[len(sums) // 2 :]
            total = sum(x.astype(F32) for x in left) + sum(x.astype(F32) for x in right)
            sums = [total.astype(BF16)]
            sums.append(swap(sums[0], mask, "pix"))
            mask *= 2
        dates_now, dates_bf = date_update(
            STEP_SCALE / all_pixels, dates_now, sums, pixel_now if last else pixel_bf
        )
        if not last:
            dates_other = swap(dates_bf, 1)
    return (pixel_now, dates_now)


def solution(mesh):
    placed = (
        P(("pix", "date"), None),
        P("date", None),
        P("pix", "date", None, None),
        P("pix", "date"),
        P("pix", "date", None, None),
        P("pix", "date", None, None),
    )
    return jax.shard_map(
        shards,
        mesh=mesh,
        in_specs=placed,
        out_specs=(P(("pix", "date"), None), P("date", None)),
        check_vma=False,
    )
```

```python
import functools

import jax
import jax.numpy as jnp
from jax import lax
from jax.experimental import pallas as pl
from jax.experimental.pallas import tpu as pltpu
from jax.sharding import PartitionSpec as P

STEPS = 2
DECAY = 0.05
STEP_SCALE = 48.0
BLOCK_ROWS = 128
BLOCK_DATES = 64
LANES = 128
GROUP = 16
F32 = jnp.float32
BF16 = jnp.bfloat16
VMEM = pl.BlockSpec(memory_space=pltpu.VMEM)
HBM = pl.BlockSpec(memory_space=pltpu.HBM)
ANY = pl.BlockSpec(memory_space=pl.ANY)
SMEM = pl.BlockSpec(memory_space=pltpu.SMEM)


def params(mib):
    return pltpu.CompilerParams(vmem_limit_bytes=mib << 20)


def cost(flops, bytes_accessed):
    return pl.CostEstimate(flops=flops, bytes_accessed=bytes_accessed, transcendentals=0)


def row_pieces(rows):
    half = BLOCK_ROWS // 2
    for block in range(rows // BLOCK_ROWS):
        for odd in range(2):
            yield block * BLOCK_ROWS + odd * half, pl.ds(block * BLOCK_ROWS + odd, half, stride=2), half


def prepare_kernel(pixel_ref, pixel_now_ref, pixel_bf_ref, slab):
    rows, rank = pixel_ref.shape
    for lane in range(0, rank, LANES):
        slab[lane // LANES] = pixel_ref[:, lane : lane + LANES]
    for to, source, half in row_pieces(rows):
        for lane in range(0, rank, LANES):
            piece = slab[lane // LANES, source, :]
            pixel_now_ref[to : to + half, lane : lane + LANES] = piece
            pixel_bf_ref[to : to + half, lane : lane + LANES] = piece.astype(BF16)


def place_kernel(copies, chip_blocks, place_ref, ids_ref, values_ref, weights_ref, panel_ref, flat, *scratch):
    slots, size = values_ref.shape
    tiles = size // LANES
    core_blocks = chip_blocks // 2
    chip, core, count = place_ref[0], place_ref[1], ids_ref[2, 0]
    spare = panel_ref.shape[1] - tiles
    refs = (values_ref, weights_ref)

    def load(g, which):
        raw, sems = scratch
        rows = pl.ds(pl.multiple_of(g * GROUP, GROUP), GROUP)
        return pltpu.make_async_copy(refs[which].at[rows], raw.at[which, rows], sems.at[which, g])

    if copies:
        for g in range(slots // GROUP):
            for which in range(2):
                load(g, which).start()
    panel_ref[...] = jnp.zeros_like(panel_ref)

    def group(g, carry):
        first = pl.multiple_of(g * GROUP, GROUP)
        if copies:
            for which in range(2):
                load(g, which).wait()

        @pl.when(first < count)
        def _():
            for which in range(2):
                source = scratch[0].at[which] if copies else refs[which]
                for t in range(tiles):
                    flat[which, t * GROUP : (t + 1) * GROUP, :] = source[
                        pl.ds(first, GROUP), t * LANES : (t + 1) * LANES
                    ].astype(F32)
            for s in range(GROUP):
                row_block, date_block = ids_ref[0, first + s], ids_ref[1, first + s]
                target = lax.bitwise_xor(lax.div(row_block, chip_blocks), chip)
                inside = lax.rem(row_block, chip_blocks)
                wanted = jnp.logical_and(lax.div(inside, core_blocks) == core, first + s < count)
                row = (target * core_blocks + lax.rem(inside, core_blocks)) * tiles
                row = pl.multiple_of(jnp.where(wanted, row, spare), tiles)
                lane = pl.multiple_of(date_block * LANES, LANES)
                for which in range(2):
                    tile = flat[which, pl.ds(s, tiles, stride=GROUP), :]
                    panel_ref[which, pl.ds(row, tiles), pl.ds(lane, LANES)] = tile.astype(BF16)

        return carry

    lax.fori_loop(0, slots // GROUP, group, 0)


def place_blocks(copies, core_blocks, place, ids, values, weights, rows, width, mib):
    slots, size = values.shape
    tiles = size // LANES
    scratch = [pltpu.VMEM((2, slots, size), BF16), pltpu.SemaphoreType.DMA((2, slots // GROUP))] if copies else []
    return pl.pallas_call(
        functools.partial(place_kernel, copies, 2 * core_blocks),
        out_shape=jax.ShapeDtypeStruct((2, rows + tiles, width), BF16),
        in_specs=[SMEM, SMEM] + [HBM if copies else VMEM] * 2,
        out_specs=VMEM,
        scratch_shapes=[pltpu.VMEM((2, tiles * GROUP, LANES), F32)] + scratch,
        compiler_params=params(mib),
        cost_estimate=cost(slots * size * 8, slots * size * 8),
    )(place, ids, values, weights)


def pack_kernel(count_ref, date_ref, ids_ref, out_ref):
    local, rank = date_ref.shape
    slots = ids_ref.shape[1]
    out_ref[:local, :] = date_ref[...].astype(BF16)
    row = lax.broadcasted_iota(jnp.int32, (GROUP, slots), 0)
    ids = jnp.where(row == 0, ids_ref[0:1, :], jnp.where(row == 1, ids_ref[1:2, :], count_ref[0, 0]))
    out_ref[local:, :] = jnp.zeros((GROUP, rank), BF16)
    out_ref[local:, :slots] = ids.astype(F32).astype(BF16)


def apart(ref, which, first, rows):
    low = lax.broadcasted_iota(jnp.int32, (rows, LANES), 1) < BLOCK_DATES
    even, odd = [], []
    for at in range(0, ref.shape[2], 2 * LANES):
        a = ref[which, first : first + rows, at : at + LANES].astype(F32)
        b = ref[which, first : first + rows, at + LANES : at + 2 * LANES].astype(F32)
        even.append(jnp.where(low, a, pltpu.roll(b, BLOCK_DATES, 1)))
        odd.append(jnp.where(low, pltpu.roll(a, BLOCK_DATES, 1), b))
    return jnp.concatenate([jnp.concatenate(even, axis=1), jnp.concatenate(odd, axis=1)], axis=0)


def chunk_kernel(n, *refs):
    pixel_refs, (dates_ref, dates_other_ref, mine_ref, other_ref) = refs[:n], refs[n : n + 4]
    term_ref, errors_ref = refs[-2:]
    half = BLOCK_ROWS // 2
    local = dates_ref.shape[0]
    blocks = pixel_refs[0].shape[0] // BLOCK_ROWS
    for block in range(n * blocks):
        inside = slice(block % blocks * BLOCK_ROWS, (block % blocks + 1) * BLOCK_ROWS)
        rows = slice(block * BLOCK_ROWS, (block + 1) * BLOCK_ROWS)
        total = None
        for k, (panel, dates) in enumerate(((mine_ref, dates_ref), (other_ref, dates_other_ref))):
            predicted = lax.dot_general(
                pixel_refs[block // blocks][inside, :], dates[...],
                (((1,), (1,)), ((), ())), preferred_element_type=F32,
            )
            observed = apart(panel, 0, block * half, half)
            weights = apart(panel, 1, block * half, half)
            errors = (weights * (predicted - observed)).astype(BF16)
            errors_ref[rows, k * local : (k + 1) * local] = errors
            term = jnp.dot(errors, dates[...], preferred_element_type=F32)
            total = term if total is None else total + term
        term_ref[rows, :] = total.astype(term_ref.dtype)


def chunk(pixels, dates_bf, dates_other, panels, at, kind, after):
    rows, rank = pixels[0].shape
    local = panels[0].shape[2] // 2
    n = len(pixels)
    whole = lambda a: pl.BlockSpec(a.shape, lambda i: (0,) * a.ndim)
    dates = pl.BlockSpec((local, rank), lambda i: (0, 0))
    panel = pl.BlockSpec((2, n * rows // 2, panels[0].shape[2]), lambda i: (0, at, 0))
    return pl.pallas_call(
        functools.partial(chunk_kernel, n),
        grid=(1,),
        out_shape=(
            jax.ShapeDtypeStruct((n * rows, rank), kind),
            jax.ShapeDtypeStruct((n * rows, 2 * local), BF16),
        ),
        in_specs=[whole(p) for p in pixels] + [dates, dates, panel, panel]
        + [ANY] * len(after),
        out_specs=(pl.BlockSpec((n * rows, rank), lambda i: (0, 0)),
                   pl.BlockSpec((n * rows, 2 * local), lambda i: (0, 0))),
        compiler_params=params(24),
        cost_estimate=cost(8 * n * rows * rank * local, n * 1200000),
    )(*pixels, dates_bf, dates_other, *panels, *after)


def hold_kernel(x_ref, *refs):
    refs[-1][...] = x_ref[...]


def hold(x, *after):
    return pl.pallas_call(
        hold_kernel,
        out_shape=jax.ShapeDtypeStruct(x.shape, x.dtype),
        in_specs=[VMEM] + [ANY] * len(after),
        out_specs=VMEM,
        compiler_params=params(16),
        cost_estimate=cost(x.size, 4 * x.size),
    )(x, *after)


def date_kernel(starts, now_ref, *refs):
    n = len(starts)
    pixel_refs, errors_refs, (own_ref, other_ref, rest_ref) = refs[:n], refs[n:-3], refs[-3:]
    rest_ref[...] = (1.0 - DECAY) * now_ref[...]
    local = own_ref.shape[0]
    for k, out in enumerate((own_ref, other_ref)):
        total = None
        for (which, start), pixels in zip(starts, pixel_refs):
            errors = errors_refs[which][start : start + pixels.shape[0], k * local : (k + 1) * local]
            term = lax.dot_general(errors, pixels[...], (((0,), (0,)), ((), ())), preferred_element_type=F32)
            total = term if total is None else total + term
        out[...] = total.astype(out.dtype)


def date_gradient(now, errors, pixels, starts):
    local, rank = now.shape
    n = len(pixels)
    return pl.pallas_call(
        functools.partial(date_kernel, starts),
        out_shape=(jax.ShapeDtypeStruct((local, rank), BF16),) * 2 + (jax.ShapeDtypeStruct((local, rank), F32),),
        in_specs=[VMEM] * (1 + n + len(errors)),
        out_specs=(VMEM, VMEM, VMEM),
        compiler_params=params(32),
        cost_estimate=cost(4 * n * pixels[0].shape[0] * rank * local, n * 400000),
    )(now, *pixels, *errors)


def sum_kernel(*refs):
    parts, out_ref = refs[:-1], refs[-1]
    total = parts[0][...].astype(F32)
    for part in parts[1:]:
        total = total + part[...].astype(F32)
    out_ref[...] = total.astype(out_ref.dtype)


def add(parts, kind):
    rows, rank = parts[0][0].shape
    block = lambda at: pl.BlockSpec((rows, rank), lambda i: (at, 0))
    return pl.pallas_call(
        sum_kernel,
        grid=(1,),
        out_shape=jax.ShapeDtypeStruct((rows, rank), kind),
        in_specs=[block(at) for _, at in parts],
        out_specs=block(0),
        compiler_params=params(16),
        cost_estimate=cost(4 * rows * rank, 8 * rows * rank),
    )(*[x for x, _ in parts])


def pixel_kernel(scale, last, now_ref, *refs):
    parts, out_ref, other_ref = refs[:2], refs[2], refs[3]
    rows, rank = now_ref.shape
    for start, target, half in row_pieces(rows):
        for lane in range(0, rank, LANES):
            at = (slice(start, start + half), slice(lane, lane + LANES))
            new = (1.0 - DECAY) * now_ref[at] - scale * (parts[0][at].astype(F32) + parts[1][at].astype(F32))
            if last:
                refs[4][lane // LANES, target, :] = new
            else:
                out_ref[at] = new
                other_ref[at] = new.astype(BF16)
    if last:
        for lane in range(0, rank, LANES):
            out_ref[:, lane : lane + LANES] = refs[4][lane // LANES]
        other_ref[...] = jnp.zeros_like(other_ref)


def pixel_update(scale, last, now, parts):
    full = jax.ShapeDtypeStruct(now.shape, F32)
    early = add([(part, 0) for part in parts[:-1]], F32)
    other = jax.ShapeDtypeStruct((8, LANES), F32) if last else jax.ShapeDtypeStruct(now.shape, BF16)
    return pl.pallas_call(
        functools.partial(pixel_kernel, scale, last),
        out_shape=(full, other),
        in_specs=[VMEM] * 3,
        out_specs=(VMEM, VMEM),
        scratch_shapes=[pltpu.VMEM((now.shape[1] // LANES, now.shape[0], LANES), F32)] if last else [],
        compiler_params=params(16),
        cost_estimate=cost(10 * now.size, 8 * now.size),
    )(now, early, parts[-1])


def date_update_kernel(scale, rest_ref, *refs):
    parts, (after_ref, new_ref, bf_ref) = refs[:-3], refs[-3:]
    halves = [None, None]
    for i, part in enumerate(parts):
        side = 2 * i // len(parts)
        value = part[...].astype(F32)
        halves[side] = value if halves[side] is None else halves[side] + value
    new = rest_ref[...] - scale * (halves[0] + halves[1])
    new_ref[...] = new
    bf_ref[...] = new.astype(BF16)


def date_update(scale, now, parts, after):
    return pl.pallas_call(
        functools.partial(date_update_kernel, scale),
        out_shape=(jax.ShapeDtypeStruct(now.shape, F32), jax.ShapeDtypeStruct(now.shape, BF16)),
        in_specs=[VMEM] * (1 + len(parts)) + [ANY],
        out_specs=(VMEM, VMEM),
        compiler_params=params(16),
        cost_estimate=cost(8 * now.size, 8 * now.size),
    )(now, *parts, after)


def shards(pixel_factors, date_factors, block_ids, block_counts, block_values, block_weights):
    loop_size, groups = lax.axis_size("date"), lax.axis_size("pix")
    own_rows, rank = pixel_factors.shape
    local = date_factors.shape[0]
    chips = loop_size // 2
    high = 4
    low = chips // high
    all_pixels = own_rows * loop_size * groups
    all_dates = local * loop_size
    slots, flat = block_values.shape[2:]
    me = lax.axis_index("date")
    tiles = flat // LANES
    core_blocks = own_rows // BLOCK_ROWS

    def swap(x, mask, axis="date"):
        return lax.ppermute(x, axis, [(i, i ^ mask) for i in range(lax.axis_size(axis))])

    shape = jax.ShapeDtypeStruct
    pixel_now, pixel_bf = pl.pallas_call(
        prepare_kernel,
        out_shape=(shape((own_rows, rank), F32), shape((own_rows, rank), BF16)),
        in_specs=[VMEM],
        out_specs=(VMEM, VMEM),
        scratch_shapes=[pltpu.VMEM((rank // LANES, own_rows, LANES), F32)],
        compiler_params=params(16),
        cost_estimate=cost(own_rows * rank, own_rows * rank * 16),
    )(pixel_factors)
    dates_now = date_factors
    block_lists = block_ids.reshape(2, slots)
    dates_bf = pl.pallas_call(
        pack_kernel,
        out_shape=shape((local + GROUP, rank), BF16),
        in_specs=[SMEM, VMEM, VMEM],
        out_specs=VMEM,
        compiler_params=params(16),
        cost_estimate=cost(local * rank, 6 * local * rank),
    )(block_counts, date_factors, block_lists)
    dates_other = swap(dates_bf, 1)

    def lists(packed):
        return packed[local : local + 3, :slots].astype(jnp.int32)

    rows, width = chips * core_blocks * tiles, local // BLOCK_DATES * LANES
    values, weights = block_values.reshape(slots, flat), block_weights.reshape(slots, flat)
    place = jnp.stack([me // 2, me % 2]).astype(jnp.int32)
    mine = place_blocks(True, core_blocks, place, lists(dates_bf), values, weights, rows, width, 36)
    other = place_blocks(
        False, core_blocks, place, lists(dates_other), swap(values, 1), swap(weights, 1), rows, width, 30
    )
    panels = (mine, other)

    for step in range(STEPS):
        last = step == STEPS - 1
        far = range(1, low)
        along = [2 * low * hi for hi in range(high)]
        pixels = {(0, 0): pixel_bf}
        pixels[3, 0] = swap(pixel_bf, along[3])
        for lo in far:
            pixels[0, lo] = swap(pixel_bf, 2 * lo)
        pixels[1, 0] = swap(pixel_bf, along[1])
        pixels[2, 0] = swap(hold(pixel_bf, pixels[1, 0] if step else pixels[0, 1], *([] if step else [mine])), along[2])
        for lo in far:
            pixels[1, lo] = swap(pixels[1, 0], 2 * lo)
            pixels[3, lo] = swap(pixels[3, 0], 2 * lo)
        errors, starts, ordered, after = [], [], [], []

        def terms(keys, kind, errors=errors, starts=starts, ordered=ordered, dates_bf=dates_bf,
                  dates_other=dates_other, pixels=pixels):
            nonlocal after
            hi, lo = keys[0]
            n = len(keys)
            term, error = chunk(
                [pixels[k] for k in keys], dates_bf, dates_other, panels, (hi * low + lo) // n, kind, after,
            )
            starts += [(len(errors), i * own_rows) for i in range(n)]
            errors.append(error)
            ordered += [pixels[k] for k in keys]
            after = [term]
            return term

        pair = terms([(1, lo) for lo in range(low)], BF16)
        for lo in far:
            pixels[2, lo] = swap(hold(pixels[2, 0], pair), 2 * lo)
        pair = swap(pair, along[1])
        recv3 = [(swap(terms([(3, lo)], BF16), 2 * lo), 0) for lo in far]
        near3 = terms([(3, 0)], F32)
        near2 = terms([(2, 0)], F32)
        near0 = terms([(0, 0)], F32)
        row0 = [terms([(0, lo)], F32) for lo in far]
        recv2 = [(swap(terms([(2, lo)], BF16), 2 * lo), 0) for lo in far]
        part3 = swap(add([(near3, 0)] + recv3, BF16), along[3])
        part0 = [swap(add([(row0[lo - 1], 0), (pair, lo)], BF16), 2 * lo) for lo in far]
        part2 = swap(add([(near2, 0)] + recv2, BF16), along[2])
        parts = [near0, pair] + part0 + [part3, part2]
        own, partner, dates_rest = date_gradient(dates_now, errors, ordered, tuple(starts))
        pixel_now, pixel_bf = pixel_update(STEP_SCALE / all_dates, last, pixel_now, parts)
        sums = [own, swap(partner, 1)]
        if groups > 1:
            count = groups * loop_size
            across = [(i, i ^ (loop_size + 1)) for i in range(count)]
            sums += [swap(own, 1, "pix"), lax.ppermute(partner, ("pix", "date"), across)]
        mask = 2
        while mask < groups:
            left, right = sums[: len(sums) // 2], sums[len(sums) // 2 :]
            total = sum(x.astype(F32) for x in left) + sum(x.astype(F32) for x in right)
            sums = [total.astype(BF16)]
            sums.append(swap(sums[0], mask, "pix"))
            mask *= 2
        dates_now, dates_bf = date_update(
            STEP_SCALE / all_pixels, dates_rest, sums, pixel_bf
        )
        if not last:
            dates_other = swap(dates_bf, 1)
    return (pixel_now, dates_now)


def solution(mesh):
    placed = (
        P(("pix", "date"), None),
        P("date", None),
        P("pix", "date", None, None),
        P("pix", "date"),
        P("pix", "date", None, None),
        P("pix", "date", None, None),
    )
    return jax.shard_map(
        shards,
        mesh=mesh,
        in_specs=placed,
        out_specs=(P(("pix", "date"), None), P("date", None)),
        check_vma=False,
    )
```

```python
import functools

import jax
import jax.numpy as jnp
from jax import lax
from jax.experimental import pallas as pl
from jax.experimental.pallas import tpu as pltpu
from jax.sharding import PartitionSpec as P

STEPS = 2
DECAY = 0.05
STEP_SCALE = 48.0
BLOCK_ROWS = 128
BLOCK_DATES = 64
LANES = 128
GROUP = 16
F32 = jnp.float32
BF16 = jnp.bfloat16
VMEM = pl.BlockSpec(memory_space=pltpu.VMEM)
HBM = pl.BlockSpec(memory_space=pltpu.HBM)
ANY = pl.BlockSpec(memory_space=pl.ANY)
SMEM = pl.BlockSpec(memory_space=pltpu.SMEM)


def params(mib):
    return pltpu.CompilerParams(vmem_limit_bytes=mib << 20)


def cost(flops, bytes_accessed):
    return pl.CostEstimate(flops=flops, bytes_accessed=bytes_accessed, transcendentals=0)


def row_pieces(rows):
    half = BLOCK_ROWS // 2
    for block in range(rows // BLOCK_ROWS):
        for odd in range(2):
            yield block * BLOCK_ROWS + odd * half, pl.ds(block * BLOCK_ROWS + odd, half, stride=2), half


def prepare_kernel(pixel_ref, pixel_bf_ref, slab):
    rows, rank = pixel_ref.shape
    for lane in range(0, rank, LANES):
        slab[lane // LANES] = pixel_ref[:, lane : lane + LANES]
    for to, source, half in row_pieces(rows):
        for lane in range(0, rank, LANES):
            pixel_bf_ref[to : to + half, lane : lane + LANES] = slab[lane // LANES, source, :].astype(BF16)


def place_kernel(copies, chip_blocks, place_ref, ids_ref, values_ref, weights_ref, panel_ref, flat, *scratch):
    slots, size = values_ref.shape
    tiles = size // LANES
    core_blocks = chip_blocks // 2
    chip, core, count = place_ref[0], place_ref[1], ids_ref[2, 0]
    spare = panel_ref.shape[1] - tiles
    refs = (values_ref, weights_ref)

    def load(g, which):
        raw, sems = scratch
        rows = pl.ds(pl.multiple_of(g * GROUP, GROUP), GROUP)
        return pltpu.make_async_copy(refs[which].at[rows], raw.at[which, rows], sems.at[which, g])

    if copies:
        for g in range(slots // GROUP):
            for which in range(2):
                load(g, which).start()
    panel_ref[...] = jnp.zeros_like(panel_ref)

    def group(g, carry):
        first = pl.multiple_of(g * GROUP, GROUP)
        if copies:
            for which in range(2):
                load(g, which).wait()

        @pl.when(first < count)
        def _():
            for which in range(2):
                source = scratch[0].at[which] if copies else refs[which]
                for t in range(tiles):
                    flat[which, t * GROUP : (t + 1) * GROUP, :] = source[
                        pl.ds(first, GROUP), t * LANES : (t + 1) * LANES
                    ].astype(F32)
            for s in range(GROUP):
                row_block, date_block = ids_ref[0, first + s], ids_ref[1, first + s]
                target = lax.bitwise_xor(lax.div(row_block, chip_blocks), chip)
                inside = lax.rem(row_block, chip_blocks)
                wanted = jnp.logical_and(lax.div(inside, core_blocks) == core, first + s < count)
                row = (target * core_blocks + lax.rem(inside, core_blocks)) * tiles
                row = pl.multiple_of(jnp.where(wanted, row, spare), tiles)
                lane = pl.multiple_of(date_block * LANES, LANES)
                for which in range(2):
                    tile = flat[which, pl.ds(s, tiles, stride=GROUP), :]
                    panel_ref[which, pl.ds(row, tiles), pl.ds(lane, LANES)] = tile.astype(BF16)

        return carry

    lax.fori_loop(0, slots // GROUP, group, 0)


def place_blocks(copies, core_blocks, place, ids, values, weights, rows, width, mib):
    slots, size = values.shape
    tiles = size // LANES
    scratch = [pltpu.VMEM((2, slots, size), BF16), pltpu.SemaphoreType.DMA((2, slots // GROUP))] if copies else []
    return pl.pallas_call(
        functools.partial(place_kernel, copies, 2 * core_blocks),
        out_shape=jax.ShapeDtypeStruct((2, rows + tiles, width), BF16),
        in_specs=[SMEM, SMEM] + [HBM if copies else VMEM] * 2,
        out_specs=VMEM,
        scratch_shapes=[pltpu.VMEM((2, tiles * GROUP, LANES), F32)] + scratch,
        compiler_params=params(mib),
        cost_estimate=cost(slots * size * 8, slots * size * 8),
    )(place, ids, values, weights)


def pack_kernel(count_ref, date_ref, ids_ref, out_ref):
    local, rank = date_ref.shape
    slots = ids_ref.shape[1]
    out_ref[:local, :] = date_ref[...].astype(BF16)
    row = lax.broadcasted_iota(jnp.int32, (GROUP, slots), 0)
    ids = jnp.where(row == 0, ids_ref[0:1, :], jnp.where(row == 1, ids_ref[1:2, :], count_ref[0, 0]))
    out_ref[local:, :] = jnp.zeros((GROUP, rank), BF16)
    out_ref[local:, :slots] = ids.astype(F32).astype(BF16)


def apart(ref, which, first, rows):
    low = lax.broadcasted_iota(jnp.int32, (rows, LANES), 1) < BLOCK_DATES
    even, odd = [], []
    for at in range(0, ref.shape[2], 2 * LANES):
        a = ref[which, first : first + rows, at : at + LANES].astype(F32)
        b = ref[which, first : first + rows, at + LANES : at + 2 * LANES].astype(F32)
        even.append(jnp.where(low, a, pltpu.roll(b, BLOCK_DATES, 1)))
        odd.append(jnp.where(low, pltpu.roll(a, BLOCK_DATES, 1), b))
    return jnp.concatenate([jnp.concatenate(even, axis=1), jnp.concatenate(odd, axis=1)], axis=0)


def chunk_kernel(n, *refs):
    pixel_refs, (dates_ref, dates_other_ref, mine_ref, other_ref) = refs[:n], refs[n : n + 4]
    term_ref, errors_ref = refs[-2:]
    half = BLOCK_ROWS // 2
    local = dates_ref.shape[0]
    blocks = pixel_refs[0].shape[0] // BLOCK_ROWS
    for block in range(n * blocks):
        inside = slice(block % blocks * BLOCK_ROWS, (block % blocks + 1) * BLOCK_ROWS)
        rows = slice(block * BLOCK_ROWS, (block + 1) * BLOCK_ROWS)
        total = None
        for k, (panel, dates) in enumerate(((mine_ref, dates_ref), (other_ref, dates_other_ref))):
            predicted = lax.dot_general(
                pixel_refs[block // blocks][inside, :], dates[...],
                (((1,), (1,)), ((), ())), preferred_element_type=F32,
            )
            observed = apart(panel, 0, block * half, half)
            weights = apart(panel, 1, block * half, half)
            errors = (weights * (predicted - observed)).astype(BF16)
            errors_ref[rows, k * local : (k + 1) * local] = errors
            term = jnp.dot(errors, dates[...], preferred_element_type=F32)
            total = term if total is None else total + term
        term_ref[rows, :] = total.astype(term_ref.dtype)


def chunk(pixels, dates_bf, dates_other, panels, at, kind, after):
    rows, rank = pixels[0].shape
    local = panels[0].shape[2] // 2
    n = len(pixels)
    whole = lambda a: pl.BlockSpec(a.shape, lambda i: (0,) * a.ndim)
    dates = pl.BlockSpec((local, rank), lambda i: (0, 0))
    panel = pl.BlockSpec((2, n * rows // 2, panels[0].shape[2]), lambda i: (0, at, 0))
    return pl.pallas_call(
        functools.partial(chunk_kernel, n),
        grid=(1,),
        out_shape=(
            jax.ShapeDtypeStruct((n * rows, rank), kind),
            jax.ShapeDtypeStruct((n * rows, 2 * local), BF16),
        ),
        in_specs=[whole(p) for p in pixels] + [dates, dates, panel, panel]
        + [ANY] * len(after),
        out_specs=(pl.BlockSpec((n * rows, rank), lambda i: (0, 0)),
                   pl.BlockSpec((n * rows, 2 * local), lambda i: (0, 0))),
        compiler_params=params(24),
        cost_estimate=cost(8 * n * rows * rank * local, n * 1200000),
    )(*pixels, dates_bf, dates_other, *panels, *after)


def hold_kernel(x_ref, *refs):
    refs[-1][...] = x_ref[...]


def hold(x, *after):
    return pl.pallas_call(
        hold_kernel,
        out_shape=jax.ShapeDtypeStruct(x.shape, x.dtype),
        in_specs=[VMEM] + [ANY] * len(after),
        out_specs=VMEM,
        compiler_params=params(16),
        cost_estimate=cost(x.size, 4 * x.size),
    )(x, *after)


def date_kernel(starts, now_ref, *refs):
    n = len(starts)
    pixel_refs, errors_refs, (own_ref, other_ref, rest_ref) = refs[:n], refs[n:-3], refs[-3:]
    rest_ref[...] = (1.0 - DECAY) * now_ref[...]
    local = own_ref.shape[0]
    for k, out in enumerate((own_ref, other_ref)):
        total = None
        for (which, start), pixels in zip(starts, pixel_refs):
            errors = errors_refs[which][start : start + pixels.shape[0], k * local : (k + 1) * local]
            term = lax.dot_general(errors, pixels[...], (((0,), (0,)), ((), ())), preferred_element_type=F32)
            total = term if total is None else total + term
        out[...] = total.astype(out.dtype)


def date_gradient(now, errors, pixels, starts):
    local, rank = now.shape
    n = len(pixels)
    return pl.pallas_call(
        functools.partial(date_kernel, starts),
        out_shape=(jax.ShapeDtypeStruct((local, rank), BF16),) * 2 + (jax.ShapeDtypeStruct((local, rank), F32),),
        in_specs=[VMEM] * (1 + n + len(errors)),
        out_specs=(VMEM, VMEM, VMEM),
        compiler_params=params(32),
        cost_estimate=cost(4 * n * pixels[0].shape[0] * rank * local, n * 400000),
    )(now, *pixels, *errors)


def sum_kernel(*refs):
    parts, out_ref = refs[:-1], refs[-1]
    total = parts[0][...].astype(F32)
    for part in parts[1:]:
        total = total + part[...].astype(F32)
    out_ref[...] = total.astype(out_ref.dtype)


def add(parts, kind):
    rows, rank = parts[0][0].shape
    block = lambda at: pl.BlockSpec((rows, rank), lambda i: (at, 0))
    return pl.pallas_call(
        sum_kernel,
        grid=(1,),
        out_shape=jax.ShapeDtypeStruct((rows, rank), kind),
        in_specs=[block(at) for _, at in parts],
        out_specs=block(0),
        compiler_params=params(16),
        cost_estimate=cost(4 * rows * rank, 8 * rows * rank),
    )(*[x for x, _ in parts])


def pixel_kernel(scale, first, last, now_ref, *refs):
    parts, out_ref, other_ref, slabs = refs[:2], refs[2], refs[3], refs[4:]
    rows, rank = now_ref.shape
    if first:
        for lane in range(0, rank, LANES):
            slabs[0][lane // LANES] = now_ref[:, lane : lane + LANES]
    for start, target, half in row_pieces(rows):
        for lane in range(0, rank, LANES):
            at = (slice(start, start + half), slice(lane, lane + LANES))
            now = slabs[0][lane // LANES, target, :] if first else now_ref[at]
            new = (1.0 - DECAY) * now - scale * (parts[0][at].astype(F32) + parts[1][at].astype(F32))
            if last:
                slabs[-1][lane // LANES, target, :] = new
            else:
                out_ref[at] = new
                other_ref[at] = new.astype(BF16)
    if last:
        for lane in range(0, rank, LANES):
            out_ref[:, lane : lane + LANES] = slabs[-1][lane // LANES]
        other_ref[...] = jnp.zeros_like(other_ref)


def pixel_update(scale, first, last, now, parts):
    full = jax.ShapeDtypeStruct(now.shape, F32)
    early = add([(part, 0) for part in parts[:-1]], F32)
    other = jax.ShapeDtypeStruct((8, LANES), F32) if last else jax.ShapeDtypeStruct(now.shape, BF16)
    return pl.pallas_call(
        functools.partial(pixel_kernel, scale, first, last),
        out_shape=(full, other),
        in_specs=[VMEM] * 3,
        out_specs=(VMEM, VMEM),
        scratch_shapes=[pltpu.VMEM((now.shape[1] // LANES, now.shape[0], LANES), F32)] * (first + last),
        compiler_params=params(16),
        cost_estimate=cost(10 * now.size, 8 * now.size),
    )(now, early, parts[-1])


def date_update_kernel(scale, rest_ref, *refs):
    parts, (after_ref, new_ref, bf_ref) = refs[:-3], refs[-3:]
    halves = [None, None]
    for i, part in enumerate(parts):
        side = 2 * i // len(parts)
        value = part[...].astype(F32)
        halves[side] = value if halves[side] is None else halves[side] + value
    new = rest_ref[...] - scale * (halves[0] + halves[1])
    new_ref[...] = new
    bf_ref[...] = new.astype(BF16)


def date_update(scale, now, parts, after):
    return pl.pallas_call(
        functools.partial(date_update_kernel, scale),
        out_shape=(jax.ShapeDtypeStruct(now.shape, F32), jax.ShapeDtypeStruct(now.shape, BF16)),
        in_specs=[VMEM] * (1 + len(parts)) + [ANY],
        out_specs=(VMEM, VMEM),
        compiler_params=params(16),
        cost_estimate=cost(8 * now.size, 8 * now.size),
    )(now, *parts, after)


def shards(pixel_factors, date_factors, block_ids, block_counts, block_values, block_weights):
    loop_size, groups = lax.axis_size("date"), lax.axis_size("pix")
    own_rows, rank = pixel_factors.shape
    local = date_factors.shape[0]
    chips = loop_size // 2
    high = 4
    low = chips // high
    all_pixels = own_rows * loop_size * groups
    all_dates = local * loop_size
    slots, flat = block_values.shape[2:]
    me = lax.axis_index("date")
    tiles = flat // LANES
    core_blocks = own_rows // BLOCK_ROWS

    def swap(x, mask, axis="date"):
        return lax.ppermute(x, axis, [(i, i ^ mask) for i in range(lax.axis_size(axis))])

    shape = jax.ShapeDtypeStruct
    pixel_now = pixel_factors
    pixel_bf = pl.pallas_call(
        prepare_kernel,
        out_shape=shape((own_rows, rank), BF16),
        in_specs=[VMEM],
        out_specs=VMEM,
        scratch_shapes=[pltpu.VMEM((rank // LANES, own_rows, LANES), F32)],
        compiler_params=params(16),
        cost_estimate=cost(own_rows * rank, own_rows * rank * 16),
    )(pixel_factors)
    dates_now = date_factors
    block_lists = block_ids.reshape(2, slots)
    dates_bf = pl.pallas_call(
        pack_kernel,
        out_shape=shape((local + GROUP, rank), BF16),
        in_specs=[SMEM, VMEM, VMEM],
        out_specs=VMEM,
        compiler_params=params(16),
        cost_estimate=cost(local * rank, 6 * local * rank),
    )(block_counts, date_factors, block_lists)
    dates_other = swap(dates_bf, 1)

    def lists(packed):
        return packed[local : local + 3, :slots].astype(jnp.int32)

    rows, width = chips * core_blocks * tiles, local // BLOCK_DATES * LANES
    values, weights = block_values.reshape(slots, flat), block_weights.reshape(slots, flat)
    place = jnp.stack([me // 2, me % 2]).astype(jnp.int32)
    mine = place_blocks(False, core_blocks, place, lists(dates_bf), values, weights, rows, width, 36)
    other = place_blocks(
        False, core_blocks, place, lists(dates_other), swap(values, 1), swap(weights, 1), rows, width, 30
    )
    panels = (mine, other)

    for step in range(STEPS):
        last = step == STEPS - 1
        far = range(1, low)
        along = [2 * low * hi for hi in range(high)]
        pixels = {(0, 0): pixel_bf}
        pixels[3, 0] = swap(pixel_bf, along[3])
        for lo in far:
            pixels[0, lo] = swap(pixel_bf, 2 * lo)
        pixels[1, 0] = swap(pixel_bf, along[1])
        pixels[2, 0] = swap(hold(pixel_bf, pixels[1, 0] if step else pixels[0, 1], *([] if step else [mine])), along[2])
        for lo in far:
            pixels[1, lo] = swap(pixels[1, 0], 2 * lo)
            pixels[3, lo] = swap(pixels[3, 0], 2 * lo)
        errors, starts, ordered, after = [], [], [], []

        def terms(keys, kind, errors=errors, starts=starts, ordered=ordered, dates_bf=dates_bf,
                  dates_other=dates_other, pixels=pixels):
            nonlocal after
            hi, lo = keys[0]
            n = len(keys)
            term, error = chunk(
                [pixels[k] for k in keys], dates_bf, dates_other, panels, (hi * low + lo) // n, kind, after,
            )
            starts += [(len(errors), i * own_rows) for i in range(n)]
            errors.append(error)
            ordered += [pixels[k] for k in keys]
            after = [term]
            return term

        pair = terms([(1, lo) for lo in range(low)], BF16)
        for lo in far:
            pixels[2, lo] = swap(hold(pixels[2, 0], pair), 2 * lo)
        pair = swap(pair, along[1])
        recv3 = [(swap(terms([(3, lo)], BF16), 2 * lo), 0) for lo in far]
        near3 = terms([(3, 0)], F32)
        near2 = terms([(2, 0)], F32)
        near0 = terms([(0, 0)], F32)
        row0 = [terms([(0, lo)], F32) for lo in far]
        recv2 = [(swap(terms([(2, lo)], BF16), 2 * lo), 0) for lo in far]
        part3 = swap(add([(near3, 0)] + recv3, BF16), along[3])
        part0 = [swap(add([(row0[lo - 1], 0), (pair, lo)], BF16), 2 * lo) for lo in far]
        part2 = swap(add([(near2, 0)] + recv2, BF16), along[2])
        parts = [near0, pair] + part0 + [part3, part2]
        own, partner, dates_rest = date_gradient(dates_now, errors, ordered, tuple(starts))
        pixel_now, pixel_bf = pixel_update(STEP_SCALE / all_dates, step == 0, last, pixel_now, parts)
        sums = [own, swap(partner, 1)]
        if groups > 1:
            count = groups * loop_size
            across = [(i, i ^ (loop_size + 1)) for i in range(count)]
            sums += [swap(own, 1, "pix"), lax.ppermute(partner, ("pix", "date"), across)]
        mask = 2
        while mask < groups:
            left, right = sums[: len(sums) // 2], sums[len(sums) // 2 :]
            total = sum(x.astype(F32) for x in left) + sum(x.astype(F32) for x in right)
            sums = [total.astype(BF16)]
            sums.append(swap(sums[0], mask, "pix"))
            mask *= 2
        dates_now, dates_bf = date_update(
            STEP_SCALE / all_pixels, dates_rest, sums, pixel_bf
        )
        if not last:
            dates_other = swap(dates_bf, 1)
    return (pixel_now, dates_now)


def solution(mesh):
    placed = (
        P(("pix", "date"), None),
        P("date", None),
        P("pix", "date", None, None),
        P("pix", "date"),
        P("pix", "date", None, None),
        P("pix", "date", None, None),
    )
    return jax.shard_map(
        shards,
        mesh=mesh,
        in_specs=placed,
        out_specs=(P(("pix", "date"), None), P("date", None)),
        check_vma=False,
    )
```
